256 devices in a mesh: rep: 16 (over z, x_lo), fsdp: 16 (over x_hi, y, core).
Axes of the slice: x: 4 (x_hi: 2, x_lo: 2; x = x_hi * 2 + x_lo), y: 4, z: 8, core: 2. Of those that a mesh axis runs over, the one named last changes fastest.
Arguments:
- activations: bfloat16 [16, 2048, 5120], P('rep', 'fsdp'), may hold values from -6 to 6
- gain: float32 [16, 5120], P('rep'), may hold values from 0.25 to 1.75
- cotangent: bfloat16 [16, 2048, 2560], P('rep', 'fsdp'), may hold values from -6 to 6
- weight: bfloat16 [16, 5120, 2560], P('rep', 'fsdp'), may hold values from -0.078125 to 0.078125
- moment1: bfloat16 [16, 5120, 2560], P('rep', 'fsdp'), may hold values from -12 to 12
- moment2: bfloat16 [16, 5120, 2560], P('rep', 'fsdp'), may hold values from 32 to 512
- step: int32 [], replicated, may hold values from 0 to 39
Outputs:
- new_weight: bfloat16 [16, 5120, 2560], P('rep', 'fsdp')
- input_gradient: bfloat16 [16, 2048, 5120], P('rep', 'fsdp')
The draws below stay inside these ranges and needn't reach their ends.
All inputs are finite; a program needn't handle non-finite values.
Results may differ from the reference program's by a relative error of at most 0.0055.
Values may be sent and summed in bfloat16 or wider, within the bound.
No kernel may reach another device: no remote copies, remote signals or barrier semaphores. Data moves between devices by JAX's collectives and lax.ppermute only.
A program may use at most 128 MiB of HBM per device.

```python
import math
import jax
import jax.numpy as jnp
from jax import lax

D = 5120
H = 2560
REPLICAS = 16
TOKENS = 2048


def block_levels(key, extent, cuts, smallest, top_value):
    factor_of, own = 1.0, jax.random.fold_in(key, 6)
    for axis_at, parts in cuts:
        steps = jnp.exp(jax.random.uniform(jax.random.fold_in(own, axis_at), (parts,), jnp.float32, smallest / len(cuts), top_value / len(cuts)))
        factor_of = factor_of * jnp.repeat(steps, extent[axis_at] // parts).reshape([-1 if axis == axis_at else 1 for axis in range(len(extent))])
    return factor_of


def centred(own_key, dims, spread, bound, shards=(), kind=jnp.bfloat16):
    factor_of = block_levels(own_key, dims, shards, -0.22, 0.18) if shards else 1.0
    array = jax.random.normal(own_key, dims, jnp.float32) * spread * factor_of
    return jnp.minimum(jnp.maximum(array, -bound), bound).astype(kind)


def setup_inputs(seed: int = 0) -> dict:
    keys = jax.random.split(jax.random.key(seed), 8)
    activations = centred(keys[0], (REPLICAS, TOKENS, D), 1.0, 6.0, ((0, 16), (1, 16)))
    gain = jnp.clip(1.0 + 0.15 * jax.random.normal(keys[1], (REPLICAS, D), jnp.float32), 0.25, 1.75)
    cotangent = centred(keys[2], (REPLICAS, TOKENS, H), 1.0, 6.0, ((0, 16), (1, 16)))
    weight = centred(keys[3], (REPLICAS, D, H), D ** -0.5, 0.078125, ((0, 16), (1, 16)))
    moment1 = centred(keys[4], (REPLICAS, D, H), 2.0, 12.0, ((0, 16), (1, 16)))
    moment2 = jnp.clip(jnp.exp(math.log(512.0) - 2.7725887 * jax.random.uniform(keys[5], (REPLICAS, D, H), jnp.float32) ** block_levels(keys[5], (REPLICAS, D, H), ((0, 16), (1, 16)), -0.2, 0.2)), 32.0, 512.0).astype(jnp.bfloat16)
    step = jax.random.randint(keys[6], (), 0, 40).astype(jnp.int32)
    return dict(activations=activations, gain=gain, cotangent=cotangent, weight=weight, moment1=moment1, moment2=moment2, step=step)


def one_replica(pieces, step):
    activations, gain, cotangent, weight, moment1, moment2 = pieces
    input_wide_float = activations.astype(jnp.float32)
    reciprocal_root_mean = lax.rsqrt(lax.optimization_barrier(jnp.mean(input_wide_float * input_wide_float, axis=-1, keepdims=True)) + 1e-05)
    normed_input = (input_wide_float * reciprocal_root_mean * gain[None, :]).astype(jnp.bfloat16)
    grad = jnp.dot(normed_input.T, cotangent, preferred_element_type=jnp.float32)
    dnormed = jnp.dot(cotangent, weight.T, preferred_element_type=jnp.float32).astype(jnp.bfloat16)
    input_hat = input_wide_float * reciprocal_root_mean
    scaled_input = gain[None, :] * dnormed.astype(jnp.float32)
    inner_product = lax.optimization_barrier(jnp.mean(scaled_input * input_hat, axis=-1, keepdims=True))
    input_gradient = (reciprocal_root_mean * (scaled_input - input_hat * inner_product)).astype(jnp.bfloat16)
    first = 0.9 * moment1.astype(jnp.float32) + 0.1 * grad
    second = 0.95 * moment2.astype(jnp.float32) + 0.05 * grad * grad
    count = (step + 1).astype(jnp.float32)
    corr_one = 1.0 - jnp.power(jnp.float32(0.9), count)
    corr_two = 1.0 - jnp.power(jnp.float32(0.95), count)
    wf = weight.astype(jnp.float32)
    updated = (wf - 0.05 * (first / corr_one / (jnp.sqrt(second / corr_two) + 1e-08) + 0.1 * wf)).astype(jnp.bfloat16)
    return (updated, input_gradient)

def reference(activations, gain, cotangent, weight, moment1, moment2, step):
    updated, input_gradient = lax.map(lambda pieces: one_replica(pieces, step), (activations, gain, cotangent, weight, moment1, moment2))
    levels = min(4, REPLICAS.bit_length() - 1)
    shift = jnp.remainder(step, levels).astype(jnp.int32)
    partner_idx = jnp.bitwise_xor(jnp.arange(REPLICAS, dtype=jnp.int32), jnp.left_shift(jnp.int32(1), shift))
    partner = jnp.take(updated, partner_idx, axis=0)
    new_weight = (0.5 * (updated.astype(jnp.float32) + partner.astype(jnp.float32))).astype(jnp.bfloat16)
    return (new_weight, input_gradient)
```

```python
from functools import partial

import jax
import jax.numpy as jnp
from jax import lax
from jax.experimental import pallas as pl
from jax.experimental.pallas import tpu as pltpu
from jax.sharding import PartitionSpec as P

BF16 = jnp.bfloat16
F32 = jnp.float32
CHIPS = 8
CHUNKS = ((0, 512), (512, 1536), (1536, 2560))
SAME_CORE = [[2 * chip + core for chip in range(CHIPS)] for core in range(2)]


def moves(dx, dy, dcore=0):
    pairs = []
    for index in range(2 * CHIPS):
        x, y, core = index >> 3, (index >> 1) & 3, index & 1
        target = (((x + dx) % 2) * 4 + (y + dy) % 4) * 2 + (core + dcore) % 2
        pairs.append((index, target))
    return pairs


def send(value, dx, dy, dcore=0):
    return lax.ppermute(value, "fsdp", moves(dx, dy, dcore))


def gossip(value, bit):
    pairs = [(source, source ^ (1 << bit)) for source in range(lax.axis_size("rep"))]
    return lax.ppermute(value, "rep", pairs)


def after(value, *others):
    return lax.optimization_barrier((value, *others))[0]


def norm_kernel(act_ref, gain_ref, out_ref):
    wide = act_ref[...].astype(F32)
    inverse = lax.rsqrt(jnp.mean(wide * wide, axis=-1, keepdims=True) + 1e-05)
    columns = out_ref.shape[1]
    for chip in range(CHIPS):
        part = pl.ds(chip * columns, columns)
        normed = act_ref[:, part].astype(F32) * inverse * gain_ref[:, part]
        out_ref[chip] = normed.T.astype(BF16)


def normed_columns(act, gain):
    tokens, width = act.shape
    return pl.pallas_call(
        norm_kernel,
        out_shape=jax.ShapeDtypeStruct((CHIPS, width // CHIPS, tokens), BF16),
        in_specs=[pl.BlockSpec(memory_space=pltpu.VMEM)] * 2,
        out_specs=pl.BlockSpec(memory_space=pltpu.VMEM),
        compiler_params=pltpu.CompilerParams(vmem_limit_bytes=32 * 2**20),
        cost_estimate=pl.CostEstimate(flops=8 * tokens * width, bytes_accessed=4 * tokens * width, transcendentals=0),
        name="norm",
    )(act, gain)


def places(coords_ref):
    x, y = coords_ref[0], coords_ref[1]
    return [
        ((x + dx) % 2) * 4 + (y + dy) % 4
        for dx, dy in ((0, 0), (1, 0), (0, 3), (1, 3), (0, 1), (1, 1), (0, 2), (1, 2))
    ]


def grad_kernel(coords_ref, normed_ref, *refs):
    pieces, (own_ref, other_ref, lhs, rhs, total, sems) = refs[:CHIPS], refs[CHIPS:]
    tokens = pieces[0].shape[0]
    copies = []
    for at in range(CHIPS):
        copies.append(
            pltpu.make_async_copy(normed_ref.at[at], lhs.at[:, pl.ds(at * tokens, tokens)], sems.at[at])
        )
    for at, block in enumerate(places(coords_ref)):
        start = pl.multiple_of(block * tokens, tokens)
        copies.append(pltpu.make_async_copy(pieces[at], rhs.at[pl.ds(start, tokens)], sems.at[CHIPS + at]))
    for copy in copies:
        copy.start()
    for copy in copies:
        copy.wait()
    rows = own_ref.shape[0]
    tile = 256
    core = coords_ref[2]

    @pl.loop(0, rhs.shape[1] // tile)
    def _(step):
        cols = pl.ds(pl.multiple_of(step * tile, tile), tile)
        total[...] = jnp.dot(lhs[...], rhs[:, cols], preferred_element_type=F32)
        own_ref[:, cols] = total[pl.ds(pl.multiple_of(core * rows, rows), rows), :]
        other_ref[:, cols] = total[pl.ds(pl.multiple_of((1 - core) * rows, rows), rows), :].astype(BF16)


def grad_chunk(coords, normed, pieces):
    tokens, width = pieces[0].shape
    columns = normed.shape[1]
    rows = columns // 2
    every = CHIPS * tokens
    vmem = pl.BlockSpec(memory_space=pltpu.VMEM)
    return pl.pallas_call(
        grad_kernel,
        out_shape=(jax.ShapeDtypeStruct((rows, width), F32), jax.ShapeDtypeStruct((rows, width), BF16)),
        in_specs=[pl.BlockSpec(memory_space=pltpu.SMEM)] + [pl.BlockSpec(memory_space=pl.ANY)] * (1 + CHIPS),
        out_specs=(vmem, vmem),
        scratch_shapes=[
            pltpu.VMEM((columns, every), BF16),
            pltpu.VMEM((every, width), BF16),
            pltpu.VMEM((columns, 256), F32),
            pltpu.SemaphoreType.DMA((2 * CHIPS,)),
        ],
        compiler_params=pltpu.CompilerParams(vmem_limit_bytes=32 * 2**20),
        cost_estimate=pl.CostEstimate(
            flops=2 * every * columns * width,
            bytes_accessed=2 * every * (columns + width) + 6 * rows * width,
            transcendentals=0,
        ),
        name="grad",
    )(coords, normed, *pieces)


def dnormed_kernel(n_chunks, spans, carried, coords_ref, mine_ref, theirs_ref, *refs):
    n_pieces = n_chunks * CHIPS
    pieces, rest = refs[:n_pieces], refs[n_pieces:]
    if carried:
        sum_ref, rest = rest[0], rest[1:]
    out_ref, lhs, rhs, sems = rest
    tokens = pieces[0].shape[0]
    rows = mine_ref.shape[0]
    core = coords_ref[2]
    first, last = spans[0][0], spans[-1][1]
    copies = []
    for which, ref in enumerate((mine_ref, theirs_ref)):
        half = core if which == 0 else 1 - core
        start = pl.multiple_of(half * rows, rows)
        copies.append(
            pltpu.make_async_copy(ref.at[:, pl.ds(first, last - first)], rhs.at[pl.ds(start, rows)], sems.at[which])
        )
    for chunk, (low, high) in enumerate(spans):
        for at, block in enumerate(places(coords_ref)):
            number = chunk * CHIPS + at
            start = pl.multiple_of(block * tokens, tokens)
            copies.append(
                pltpu.make_async_copy(
                    pieces[number],
                    lhs.at[pl.ds(start, tokens), pl.ds(low - first, high - low)],
                    sems.at[2 + number],
                )
            )
    for copy in copies:
        copy.start()
    for copy in copies:
        copy.wait()

    @pl.loop(0, CHIPS // 2)
    def _(step):
        these = pl.ds(pl.multiple_of(step * 2 * tokens, 2 * tokens), 2 * tokens)
        part = lax.dot_general(lhs[these, :], rhs[...], (((1,), (1,)), ((), ())), preferred_element_type=F32)
        part = part.reshape(2, tokens, 2 * rows)
        blocks = pl.ds(step * 2, 2)
        if carried:
            part = part + sum_ref[blocks]
        out_ref[blocks] = part.astype(out_ref.dtype)


def dnormed_part(coords, mine, theirs, chunks, spans, carry, dtype):
    tokens = chunks[0][0].shape[0]
    rows = mine.shape[0]
    depth = spans[-1][1] - spans[0][0]
    pieces = [piece for chunk in chunks for piece in chunk]
    every = CHIPS * tokens
    vmem = pl.BlockSpec(memory_space=pltpu.VMEM)
    carried = [] if carry is None else [carry]
    return pl.pallas_call(
        partial(dnormed_kernel, len(chunks), spans, bool(carried)),
        out_shape=jax.ShapeDtypeStruct((CHIPS, tokens, 2 * rows), dtype),
        in_specs=[pl.BlockSpec(memory_space=pltpu.SMEM)]
        + [pl.BlockSpec(memory_space=pl.ANY)] * (2 + len(pieces))
        + [vmem] * len(carried),
        out_specs=vmem,
        scratch_shapes=[
            pltpu.VMEM((every, depth), BF16),
            pltpu.VMEM((2 * rows, depth), BF16),
            pltpu.SemaphoreType.DMA((2 + len(pieces),)),
        ],
        compiler_params=pltpu.CompilerParams(vmem_limit_bytes=32 * 2**20),
        cost_estimate=pl.CostEstimate(
            flops=4 * every * rows * depth,
            bytes_accessed=2 * (every + 2 * rows) * depth + 8 * every * rows,
            transcendentals=0,
        ),
        name="dnormed",
    )(coords, mine, theirs, *pieces, *carried)


def input_kernel(act_ref, gain_ref, dn_ref, out_ref):
    width = act_ref.shape[1]
    columns = dn_ref.shape[2]
    square = dot = 0.0
    for chip in range(CHIPS):
        part = pl.ds(chip * columns, columns)
        wide = act_ref[:, part].astype(F32)
        scaled = gain_ref[:, part] * dn_ref[chip].astype(F32)
        square = square + jnp.sum(wide * wide, axis=-1, keepdims=True)
        dot = dot + jnp.sum(scaled * wide, axis=-1, keepdims=True)
    inverse = lax.rsqrt(square / width + 1e-05)
    inner = inverse * dot / width
    for chip in range(CHIPS):
        part = pl.ds(chip * columns, columns)
        hat = act_ref[:, part].astype(F32) * inverse
        scaled = gain_ref[:, part] * dn_ref[chip].astype(F32)
        out_ref[:, part] = (inverse * (scaled - hat * inner)).astype(BF16)


def input_gradients(act, gain, dn):
    tokens, width = act.shape
    step = 32
    return pl.pallas_call(
        input_kernel,
        grid=(tokens // step,),
        out_shape=jax.ShapeDtypeStruct((tokens, width), BF16),
        in_specs=[
            pl.BlockSpec((step, width), lambda i: (i, 0)),
            pl.BlockSpec((1, width), lambda i: (0, 0)),
            pl.BlockSpec((CHIPS, step, width // CHIPS), lambda i: (0, i, 0)),
        ],
        out_specs=pl.BlockSpec((step, width), lambda i: (i, 0)),
        compiler_params=pltpu.CompilerParams(vmem_limit_bytes=32 * 2**20),
        cost_estimate=pl.CostEstimate(flops=12 * tokens * width, bytes_accessed=6 * tokens * width, transcendentals=0),
        name="input_gradient",
    )(act, gain, dn)


def gather_chunk(own):
    across = send(own, 1, 0)
    below = send(own, 0, 1)
    above = send(own, 0, 3)
    below_across = send(across, 0, 1)
    above_across = send(across, 0, 3)
    far = send(below, 0, 1)
    far_across = send(above_across, 0, 3)
    return (own, across, below, below_across, above, above_across, far, far_across)


def exchange(value):
    return lax.all_to_all(
        value, "fsdp", split_axis=0, concat_axis=0, tiled=True, axis_index_groups=SAME_CORE
    )


def whole(bit, act, gain, cot, weight, moment1, moment2, corr_one, corr_two, coords):
    normed = exchange(normed_columns(act, gain))
    weight_theirs = send(weight, 0, 0, 1)
    chunks = []
    previous = None
    for low, high in CHUNKS:
        own = cot[:, low:high]
        if previous is not None:
            own = after(own, *previous[1:3])
        previous = gather_chunk(own)
        chunks.append(previous)
    results = []
    for (low, high), pieces in zip(CHUNKS, chunks):
        mine, theirs = grad_chunk(coords, normed, pieces)
        grad = mine + send(theirs, 0, 0, 1).astype(F32)
        first = 0.9 * moment1[:, low:high].astype(F32) + 0.1 * grad
        second = 0.95 * moment2[:, low:high].astype(F32) + 0.05 * grad * grad
        wide = weight[:, low:high].astype(F32)
        updated = (
            wide - 0.05 * (first / corr_one / (jnp.sqrt(second / corr_two) + 1e-08) + 0.1 * wide)
        ).astype(BF16)
        results.append((updated, gossip(updated, bit)))
    carry = dnormed_part(coords, weight, weight_theirs, chunks[:2], CHUNKS[:2], None, F32)
    dn = dnormed_part(coords, weight, weight_theirs, chunks[2:], CHUNKS[2:], carry, BF16)
    input_gradient = input_gradients(act, gain, exchange(dn))
    new_weight = jnp.concatenate(
        [(0.5 * (mine.astype(F32) + theirs.astype(F32))).astype(BF16) for mine, theirs in results], axis=1
    )
    return new_weight[None], input_gradient[None]


def on_device(activations, gain, cotangent, weight, moment1, moment2, step):
    index = lax.axis_index("fsdp")
    coords = jnp.stack([index // 8, (index // 2) % 4, index % 2]).astype(jnp.int32)
    count = (step + 1).astype(F32)
    corr_one = 1.0 - jnp.power(F32(0.9), count)
    corr_two = 1.0 - jnp.power(F32(0.95), count)
    levels = min(4, lax.axis_size("rep").bit_length() - 1)
    which = jnp.remainder(step, levels)
    return lax.switch(
        which,
        [partial(whole, bit) for bit in range(levels)],
        activations[0],
        gain,
        cotangent[0],
        weight[0],
        moment1[0],
        moment2[0],
        corr_one,
        corr_two,
        coords,
    )


def solution(mesh):
    placed = (
        P("rep", "fsdp", None),
        P("rep", None),
        P("rep", "fsdp", None),
        P("rep", "fsdp", None),
        P("rep", "fsdp", None),
        P("rep", "fsdp", None),
        P(),
    )
    return jax.shard_map(
        on_device,
        mesh=mesh,
        in_specs=placed,
        out_specs=(P("rep", "fsdp", None), P("rep", "fsdp", None)),
        check_vma=False,
    )
```

```python
from functools import partial

import jax
import jax.numpy as jnp
from jax import lax
from jax.experimental import pallas as pl
from jax.experimental.pallas import tpu as pltpu
from jax.sharding import PartitionSpec as P

BF16 = jnp.bfloat16
F32 = jnp.float32
CHIPS = 8
CHUNKS = ((0, 1536), (1536, 2560))
SAME_CORE = [[2 * chip + core for chip in range(CHIPS)] for core in range(2)]


def moves(dx, dy, dcore=0):
    pairs = []
    for index in range(2 * CHIPS):
        x, y, core = index >> 3, (index >> 1) & 3, index & 1
        target = (((x + dx) % 2) * 4 + (y + dy) % 4) * 2 + (core + dcore) % 2
        pairs.append((index, target))
    return pairs


def send(value, dx, dy, dcore=0):
    return lax.ppermute(value, "fsdp", moves(dx, dy, dcore))


def gossip(value, bit):
    pairs = [(source, source ^ (1 << bit)) for source in range(lax.axis_size("rep"))]
    return lax.ppermute(value, "rep", pairs)


def after(value, *others):
    return lax.optimization_barrier((value, *others))[0]


def norm_kernel(act_ref, gain_ref, out_ref):
    wide = act_ref[...].astype(F32)
    inverse = lax.rsqrt(jnp.mean(wide * wide, axis=-1, keepdims=True) + 1e-05)
    columns = out_ref.shape[1]
    for chip in range(CHIPS):
        part = pl.ds(chip * columns, columns)
        normed = act_ref[:, part].astype(F32) * inverse * gain_ref[:, part]
        out_ref[chip] = normed.T.astype(BF16)


def normed_columns(act, gain):
    tokens, width = act.shape
    return pl.pallas_call(
        norm_kernel,
        out_shape=jax.ShapeDtypeStruct((CHIPS, width // CHIPS, tokens), BF16),
        in_specs=[pl.BlockSpec(memory_space=pltpu.VMEM)] * 2,
        out_specs=pl.BlockSpec(memory_space=pltpu.VMEM),
        compiler_params=pltpu.CompilerParams(vmem_limit_bytes=10 * 2**20),
        cost_estimate=pl.CostEstimate(flops=8 * tokens * width, bytes_accessed=4 * tokens * width, transcendentals=0),
        name="norm",
    )(act, gain)


def places(coords_ref):
    x, y = coords_ref[0], coords_ref[1]
    return [
        ((x + dx) % 2) * 4 + (y + dy) % 4
        for dx, dy in ((0, 0), (1, 0), (0, 3), (1, 3), (0, 1), (1, 1), (0, 2), (1, 2))
    ]


def grad_kernel(coords_ref, normed_ref, *refs):
    pieces, (own_ref, other_ref, lhs, rhs, total, sems) = refs[:CHIPS], refs[CHIPS:]
    tokens = pieces[0].shape[0]
    copies = []
    for at in range(CHIPS):
        copies.append(
            pltpu.make_async_copy(normed_ref.at[at], lhs.at[:, pl.ds(at * tokens, tokens)], sems.at[at])
        )
    for at, block in enumerate(places(coords_ref)):
        start = pl.multiple_of(block * tokens, tokens)
        copies.append(pltpu.make_async_copy(pieces[at], rhs.at[pl.ds(start, tokens)], sems.at[CHIPS + at]))
    for copy in copies:
        copy.start()
    for copy in copies:
        copy.wait()
    rows = own_ref.shape[0]
    tile = 256
    core = coords_ref[2]

    @pl.loop(0, rhs.shape[1] // tile)
    def _(step):
        cols = pl.ds(pl.multiple_of(step * tile, tile), tile)
        total[...] = jnp.dot(lhs[...], rhs[:, cols], preferred_element_type=F32)
        own_ref[:, cols] = total[pl.ds(pl.multiple_of(core * rows, rows), rows), :]
        other_ref[:, cols] = total[pl.ds(pl.multiple_of((1 - core) * rows, rows), rows), :].astype(BF16)


def grad_chunk(coords, normed, pieces):
    tokens, width = pieces[0].shape
    columns = normed.shape[1]
    rows = columns // 2
    every = CHIPS * tokens
    vmem = pl.BlockSpec(memory_space=pltpu.VMEM)
    return pl.pallas_call(
        grad_kernel,
        out_shape=(jax.ShapeDtypeStruct((rows, width), F32), jax.ShapeDtypeStruct((rows, width), BF16)),
        in_specs=[pl.BlockSpec(memory_space=pltpu.SMEM)] + [pl.BlockSpec(memory_space=pltpu.HBM)] * (1 + CHIPS),
        out_specs=(vmem, vmem),
        scratch_shapes=[
            pltpu.VMEM((columns, every), BF16),
            pltpu.VMEM((every, width), BF16),
            pltpu.VMEM((columns, 256), F32),
            pltpu.SemaphoreType.DMA((2 * CHIPS,)),
        ],
        compiler_params=pltpu.CompilerParams(vmem_limit_bytes=16 * 2**20),
        cost_estimate=pl.CostEstimate(
            flops=2 * every * columns * width,
            bytes_accessed=2 * every * (columns + width) + 6 * rows * width,
            transcendentals=0,
        ),
        name="grad",
    )(coords, normed, *pieces)


def dnormed_kernel(n_chunks, spans, carried, coords_ref, mine_ref, theirs_ref, *refs):
    n_pieces = n_chunks * CHIPS
    pieces, rest = refs[:n_pieces], refs[n_pieces:]
    if carried:
        sum_ref, rest = rest[0], rest[1:]
    out_ref, lhs, rhs, sems = rest
    tokens = pieces[0].shape[0]
    rows = mine_ref.shape[0]
    core = coords_ref[2]
    first, last = spans[0][0], spans[-1][1]
    copies = []
    for which, ref in enumerate((mine_ref, theirs_ref)):
        half = core if which == 0 else 1 - core
        start = pl.multiple_of(half * rows, rows)
        copies.append(
            pltpu.make_async_copy(ref.at[:, pl.ds(first, last - first)], rhs.at[pl.ds(start, rows)], sems.at[which])
        )
    for chunk, (low, high) in enumerate(spans):
        for at, block in enumerate(places(coords_ref)):
            number = chunk * CHIPS + at
            start = pl.multiple_of(block * tokens, tokens)
            copies.append(
                pltpu.make_async_copy(
                    pieces[number],
                    lhs.at[pl.ds(start, tokens), pl.ds(low - first, high - low)],
                    sems.at[2 + number],
                )
            )
    for copy in copies:
        copy.start()
    for copy in copies:
        copy.wait()

    @pl.loop(0, CHIPS // 2)
    def _(step):
        these = pl.ds(pl.multiple_of(step * 2 * tokens, 2 * tokens), 2 * tokens)
        part = lax.dot_general(lhs[these, :], rhs[...], (((1,), (1,)), ((), ())), preferred_element_type=F32)
        part = part.reshape(2, tokens, 2 * rows)
        blocks = pl.ds(step * 2, 2)
        if carried:
            part = part + sum_ref[blocks]
        out_ref[blocks] = part.astype(out_ref.dtype)


def dnormed_part(coords, mine, theirs, chunks, spans, carry, dtype):
    tokens = chunks[0][0].shape[0]
    rows = mine.shape[0]
    depth = spans[-1][1] - spans[0][0]
    pieces = [piece for chunk in chunks for piece in chunk]
    every = CHIPS * tokens
    vmem = pl.BlockSpec(memory_space=pltpu.VMEM)
    carried = [] if carry is None else [carry]
    return pl.pallas_call(
        partial(dnormed_kernel, len(chunks), spans, bool(carried)),
        out_shape=jax.ShapeDtypeStruct((CHIPS, tokens, 2 * rows), dtype),
        in_specs=[pl.BlockSpec(memory_space=pltpu.SMEM)]
        + [pl.BlockSpec(memory_space=pltpu.HBM)] * (2 + len(pieces))
        + [vmem] * len(carried),
        out_specs=vmem,
        scratch_shapes=[
            pltpu.VMEM((every, depth), BF16),
            pltpu.VMEM((2 * rows, depth), BF16),
            pltpu.SemaphoreType.DMA((2 + len(pieces),)),
        ],
        compiler_params=pltpu.CompilerParams(vmem_limit_bytes=16 * 2**20),
        cost_estimate=pl.CostEstimate(
            flops=4 * every * rows * depth,
            bytes_accessed=2 * (every + 2 * rows) * depth + 8 * every * rows,
            transcendentals=0,
        ),
        name="dnormed",
    )(coords, mine, theirs, *pieces, *carried)


def input_kernel(act_ref, gain_ref, dn_ref, out_ref):
    width = act_ref.shape[1]
    columns = dn_ref.shape[2]
    square = dot = 0.0
    for chip in range(CHIPS):
        part = pl.ds(chip * columns, columns)
        wide = act_ref[:, part].astype(F32)
        scaled = gain_ref[:, part] * dn_ref[chip].astype(F32)
        square = square + jnp.sum(wide * wide, axis=-1, keepdims=True)
        dot = dot + jnp.sum(scaled * wide, axis=-1, keepdims=True)
    inverse = lax.rsqrt(square / width + 1e-05)
    inner = inverse * dot / width
    for chip in range(CHIPS):
        part = pl.ds(chip * columns, columns)
        hat = act_ref[:, part].astype(F32) * inverse
        scaled = gain_ref[:, part] * dn_ref[chip].astype(F32)
        out_ref[:, part] = (inverse * (scaled - hat * inner)).astype(BF16)


def input_gradients(act, gain, dn):
    tokens, width = act.shape
    step = 32
    return pl.pallas_call(
        input_kernel,
        grid=(tokens // step,),
        out_shape=jax.ShapeDtypeStruct((tokens, width), BF16),
        in_specs=[
            pl.BlockSpec((step, width), lambda i: (i, 0)),
            pl.BlockSpec((1, width), lambda i: (0, 0)),
            pl.BlockSpec((CHIPS, step, width // CHIPS), lambda i: (0, i, 0)),
        ],
        out_specs=pl.BlockSpec((step, width), lambda i: (i, 0)),
        compiler_params=pltpu.CompilerParams(vmem_limit_bytes=8 * 2**20),
        cost_estimate=pl.CostEstimate(flops=12 * tokens * width, bytes_accessed=6 * tokens * width, transcendentals=0),
        name="input_gradient",
    )(act, gain, dn)


def average_kernel(spans, *refs):
    out_ref = refs[-1]
    for number, (low, high) in enumerate(spans):
        mine, theirs = refs[2 * number][...].astype(F32), refs[2 * number + 1][...].astype(F32)
        out_ref[:, low:high] = (0.5 * (mine + theirs)).astype(BF16)


def average(spans, pairs):
    rows, width = pairs[0][0].shape[0], spans[-1][1]
    step = 80
    values = [value for pair in pairs for value in pair]
    return pl.pallas_call(
        partial(average_kernel, spans),
        grid=(rows // step,),
        out_shape=jax.ShapeDtypeStruct((rows, width), BF16),
        in_specs=[pl.BlockSpec((step, value.shape[1]), lambda i: (i, 0)) for value in values],
        out_specs=pl.BlockSpec((step, width), lambda i: (i, 0)),
        compiler_params=pltpu.CompilerParams(vmem_limit_bytes=8 * 2**20),
        cost_estimate=pl.CostEstimate(flops=2 * rows * width, bytes_accessed=6 * rows * width, transcendentals=0),
        name="average",
    )(*values)


def first_hops(own):
    return own, send(own, 1, 0), send(own, 0, 1), send(own, 0, 3)


def other_hops(own, across, below, above):
    below_across = send(across, 0, 1)
    above_across = send(across, 0, 3)
    far = send(below, 0, 1)
    far_across = send(above_across, 0, 3)
    return (own, across, below, below_across, above, above_across, far, far_across)


def exchange(value):
    return lax.all_to_all(
        value, "fsdp", split_axis=0, concat_axis=0, tiled=True, axis_index_groups=SAME_CORE
    )


def update(span, mine, theirs, weight, moment1, moment2, corr_one, corr_two):
    columns = slice(*span)
    grad = mine + theirs.astype(F32)
    first = 0.9 * moment1[:, columns].astype(F32) + 0.1 * grad
    second = 0.95 * moment2[:, columns].astype(F32) + 0.05 * grad * grad
    wide = weight[:, columns].astype(F32)
    return (
        wide - 0.05 * (first / corr_one / (jnp.sqrt(second / corr_two) + 1e-08) + 0.1 * wide)
    ).astype(BF16)


def before_gossip(act, gain, cot, weight, moment1, moment2, corr_one, corr_two, coords):
    start = first_hops(cot[:, slice(*CHUNKS[0])])
    normed = exchange(normed_columns(act, gain))
    weight_theirs = send(weight, 0, 0, 1)
    pieces = other_hops(*start)
    later = other_hops(*first_hops(after(cot[:, slice(*CHUNKS[1])], *start[1:])))
    mine, theirs = grad_chunk(coords, after(normed, *later[1:3], later[4]), pieces)
    swapped = send(theirs, 0, 0, 1)
    updated = update(CHUNKS[0], mine, swapped, weight, moment1, moment2, corr_one, corr_two)
    held = (after(pieces[0], theirs),) + pieces[1:]
    carry = dnormed_part(coords, weight, weight_theirs, [held], CHUNKS[:1], None, F32)
    return normed, later, weight_theirs, updated, carry


def with_gossip(
    bit, normed, pieces, weight_theirs, updated, carry, act, gain, weight, moment1, moment2, corr_one, corr_two, coords
):
    partner = gossip(updated, bit)
    mine, theirs = grad_chunk(coords, normed, pieces)
    swapped = send(theirs, 0, 0, 1)
    held = (after(pieces[0], theirs),) + pieces[1:]
    dn = dnormed_part(coords, weight, weight_theirs, [held], CHUNKS[1:], carry, BF16)
    updated_later = update(CHUNKS[1], mine, swapped, weight, moment1, moment2, corr_one, corr_two)
    partner_later = gossip(after(updated_later, partner), bit)
    input_gradient = input_gradients(act, gain, exchange(dn))
    new_weight = average(CHUNKS, [(updated, partner), (updated_later, partner_later)])
    return new_weight[None], input_gradient[None]


def on_device(activations, gain, cotangent, weight, moment1, moment2, step):
    index = lax.axis_index("fsdp")
    coords = jnp.stack([index // 8, (index // 2) % 4, index % 2]).astype(jnp.int32)
    count = (step + 1).astype(F32)
    corr_one = 1.0 - jnp.power(F32(0.9), count)
    corr_two = 1.0 - jnp.power(F32(0.95), count)
    levels = min(4, lax.axis_size("rep").bit_length() - 1)
    which = jnp.remainder(step, levels)
    act, cot, weight = activations[0], cotangent[0], weight[0]
    rest = (weight, moment1[0], moment2[0], corr_one, corr_two, coords)
    ready = before_gossip(act, gain, cot, *rest)
    return lax.switch(
        which, [partial(with_gossip, bit) for bit in range(levels)], *ready, act, gain, *rest
    )


def solution(mesh):
    placed = (
        P("rep", "fsdp", None),
        P("rep", None),
        P("rep", "fsdp", None),
        P("rep", "fsdp", None),
        P("rep", "fsdp", None),
        P("rep", "fsdp", None),
        P(),
    )
    return jax.shard_map(
        on_device,
        mesh=mesh,
        in_specs=placed,
        out_specs=(P("rep", "fsdp", None), P("rep", "fsdp", None)),
        check_vma=False,
    )
```

```python
from functools import partial

import jax
import jax.numpy as jnp
from jax import lax
from jax.experimental import pallas as pl
from jax.experimental.pallas import tpu as pltpu
from jax.sharding import PartitionSpec as P

BF16 = jnp.bfloat16
F32 = jnp.float32
CHIPS = 8
SAME_CORE = [[2 * chip + core for chip in range(CHIPS)] for core in range(2)]


def moves(dx, dy, dcore=0):
    pairs = []
    for index in range(2 * CHIPS):
        x, y, core = index >> 3, (index >> 1) & 3, index & 1
        target = (((x + dx) % 2) * 4 + (y + dy) % 4) * 2 + (core + dcore) % 2
        pairs.append((index, target))
    return pairs


def send(value, dx, dy, dcore=0):
    return lax.ppermute(value, "fsdp", moves(dx, dy, dcore))


def gossip(value, bit):
    pairs = [(source, source ^ (1 << bit)) for source in range(lax.axis_size("rep"))]
    return lax.ppermute(value, "rep", pairs)


def after(value, *others):
    return lax.optimization_barrier((value, *others))[0]


def norm_kernel(act_ref, gain_ref, out_ref):
    wide = act_ref[...].astype(F32)
    inverse = lax.rsqrt(jnp.mean(wide * wide, axis=-1, keepdims=True) + 1e-05)
    columns = out_ref.shape[1]
    for chip in range(CHIPS):
        part = pl.ds(chip * columns, columns)
        normed = act_ref[:, part].astype(F32) * inverse * gain_ref[:, part]
        out_ref[chip] = normed.T.astype(BF16)


def normed_columns(act, gain):
    tokens, width = act.shape
    return pl.pallas_call(
        norm_kernel,
        out_shape=jax.ShapeDtypeStruct((CHIPS, width // CHIPS, tokens), BF16),
        in_specs=[pl.BlockSpec(memory_space=pltpu.VMEM)] * 2,
        out_specs=pl.BlockSpec(memory_space=pltpu.VMEM),
        compiler_params=pltpu.CompilerParams(vmem_limit_bytes=10 * 2**20),
        cost_estimate=pl.CostEstimate(flops=8 * tokens * width, bytes_accessed=4 * tokens * width, transcendentals=0),
        name="norm",
    )(act, gain)


def places(coords_ref):
    x, y = coords_ref[0], coords_ref[1]
    return [
        ((x + dx) % 2) * 4 + (y + dy) % 4
        for dx, dy in ((0, 0), (1, 0), (0, 3), (1, 3), (0, 1), (1, 1), (0, 2), (1, 2))
    ]


def grad_kernel(coords_ref, normed_ref, *refs):
    pieces, (own_ref, other_ref, lhs, rhs, total, sems) = refs[:CHIPS], refs[CHIPS:]
    tokens = pieces[0].shape[0]
    copies = []
    for at in range(CHIPS):
        copies.append(
            pltpu.make_async_copy(normed_ref.at[at], lhs.at[:, pl.ds(at * tokens, tokens)], sems.at[at])
        )
    for at, block in enumerate(places(coords_ref)):
        start = pl.multiple_of(block * tokens, tokens)
        copies.append(pltpu.make_async_copy(pieces[at], rhs.at[pl.ds(start, tokens)], sems.at[CHIPS + at]))
    for copy in copies:
        copy.start()
    for copy in copies:
        copy.wait()
    rows = own_ref.shape[0]
    tile = 256
    core = coords_ref[2]

    @pl.loop(0, rhs.shape[1] // tile)
    def _(step):
        cols = pl.ds(pl.multiple_of(step * tile, tile), tile)
        total[...] = jnp.dot(lhs[...], rhs[:, cols], preferred_element_type=F32)
        own_ref[:, cols] = total[pl.ds(pl.multiple_of(core * rows, rows), rows), :]
        other_ref[:, cols] = total[pl.ds(pl.multiple_of((1 - core) * rows, rows), rows), :].astype(BF16)


def grad_chunk(coords, normed, pieces):
    tokens, width = pieces[0].shape
    columns = normed.shape[1]
    rows = columns // 2
    every = CHIPS * tokens
    vmem = pl.BlockSpec(memory_space=pltpu.VMEM)
    return pl.pallas_call(
        grad_kernel,
        out_shape=(jax.ShapeDtypeStruct((rows, width), F32), jax.ShapeDtypeStruct((rows, width), BF16)),
        in_specs=[pl.BlockSpec(memory_space=pltpu.SMEM)] + [pl.BlockSpec(memory_space=pltpu.HBM)] * (1 + CHIPS),
        out_specs=(vmem, vmem),
        scratch_shapes=[
            pltpu.VMEM((columns, every), BF16),
            pltpu.VMEM((every, width), BF16),
            pltpu.VMEM((columns, 256), F32),
            pltpu.SemaphoreType.DMA((2 * CHIPS,)),
        ],
        compiler_params=pltpu.CompilerParams(vmem_limit_bytes=24 * 2**20),
        cost_estimate=pl.CostEstimate(
            flops=2 * every * columns * width,
            bytes_accessed=2 * every * (columns + width) + 6 * rows * width,
            transcendentals=0,
        ),
        name="grad",
    )(coords, normed, *pieces)


def dnormed_kernel(n_chunks, spans, carried, coords_ref, mine_ref, theirs_ref, *refs):
    n_pieces = n_chunks * CHIPS
    pieces, rest = refs[:n_pieces], refs[n_pieces:]
    if carried:
        sum_ref, rest = rest[0], rest[1:]
    out_ref, lhs, rhs, sems = rest
    tokens = pieces[0].shape[0]
    rows = mine_ref.shape[0]
    core = coords_ref[2]
    first, last = spans[0][0], spans[-1][1]
    copies = []
    for which, ref in enumerate((mine_ref, theirs_ref)):
        half = core if which == 0 else 1 - core
        start = pl.multiple_of(half * rows, rows)
        copies.append(
            pltpu.make_async_copy(ref.at[:, pl.ds(first, last - first)], rhs.at[pl.ds(start, rows)], sems.at[which])
        )
    for chunk, (low, high) in enumerate(spans):
        for at, block in enumerate(places(coords_ref)):
            number = chunk * CHIPS + at
            start = pl.multiple_of(block * tokens, tokens)
            copies.append(
                pltpu.make_async_copy(
                    pieces[number],
                    lhs.at[pl.ds(start, tokens), pl.ds(low - first, high - low)],
                    sems.at[2 + number],
                )
            )
    for copy in copies:
        copy.start()
    for copy in copies:
        copy.wait()

    @pl.loop(0, CHIPS // 2)
    def _(step):
        these = pl.ds(pl.multiple_of(step * 2 * tokens, 2 * tokens), 2 * tokens)
        part = lax.dot_general(lhs[these, :], rhs[...], (((1,), (1,)), ((), ())), preferred_element_type=F32)
        part = part.reshape(2, tokens, 2 * rows)
        blocks = pl.ds(step * 2, 2)
        if carried:
            part = part + sum_ref[blocks]
        out_ref[blocks] = part.astype(out_ref.dtype)


def dnormed_part(coords, mine, theirs, chunks, spans, carry, dtype):
    tokens = chunks[0][0].shape[0]
    rows = mine.shape[0]
    depth = spans[-1][1] - spans[0][0]
    pieces = [piece for chunk in chunks for piece in chunk]
    every = CHIPS * tokens
    vmem = pl.BlockSpec(memory_space=pltpu.VMEM)
    carried = [] if carry is None else [carry]
    return pl.pallas_call(
        partial(dnormed_kernel, len(chunks), spans, bool(carried)),
        out_shape=jax.ShapeDtypeStruct((CHIPS, tokens, 2 * rows), dtype),
        in_specs=[pl.BlockSpec(memory_space=pltpu.SMEM)]
        + [pl.BlockSpec(memory_space=pltpu.HBM)] * (2 + len(pieces))
        + [vmem] * len(carried),
        out_specs=vmem,
        scratch_shapes=[
            pltpu.VMEM((every, depth), BF16),
            pltpu.VMEM((2 * rows, depth), BF16),
            pltpu.SemaphoreType.DMA((2 + len(pieces),)),
        ],
        compiler_params=pltpu.CompilerParams(vmem_limit_bytes=20 * 2**20),
        cost_estimate=pl.CostEstimate(
            flops=4 * every * rows * depth,
            bytes_accessed=2 * (every + 2 * rows) * depth + 8 * every * rows,
            transcendentals=0,
        ),
        name="dnormed",
    )(coords, mine, theirs, *pieces, *carried)


def input_kernel(act_ref, gain_ref, dn_ref, out_ref):
    width = act_ref.shape[1]
    columns = dn_ref.shape[2]
    square = dot = 0.0
    for chip in range(CHIPS):
        part = pl.ds(chip * columns, columns)
        wide = act_ref[:, part].astype(F32)
        scaled = gain_ref[:, part] * dn_ref[chip].astype(F32)
        square = square + jnp.sum(wide * wide, axis=-1, keepdims=True)
        dot = dot + jnp.sum(scaled * wide, axis=-1, keepdims=True)
    inverse = lax.rsqrt(square / width + 1e-05)
    inner = inverse * dot / width
    for chip in range(CHIPS):
        part = pl.ds(chip * columns, columns)
        hat = act_ref[:, part].astype(F32) * inverse
        scaled = gain_ref[:, part] * dn_ref[chip].astype(F32)
        out_ref[:, part] = (inverse * (scaled - hat * inner)).astype(BF16)


def input_gradients(act, gain, dn):
    tokens, width = act.shape
    step = 32
    return pl.pallas_call(
        input_kernel,
        grid=(tokens // step,),
        out_shape=jax.ShapeDtypeStruct((tokens, width), BF16),
        in_specs=[
            pl.BlockSpec((step, width), lambda i: (i, 0)),
            pl.BlockSpec((1, width), lambda i: (0, 0)),
            pl.BlockSpec((CHIPS, step, width // CHIPS), lambda i: (0, i, 0)),
        ],
        out_specs=pl.BlockSpec((step, width), lambda i: (i, 0)),
        compiler_params=pltpu.CompilerParams(vmem_limit_bytes=8 * 2**20),
        cost_estimate=pl.CostEstimate(flops=12 * tokens * width, bytes_accessed=6 * tokens * width, transcendentals=0),
        name="input_gradient",
    )(act, gain, dn)


def first_hops(own):
    return own, send(own, 1, 0), send(own, 0, 1), send(own, 0, 3)


def other_hops(own, across, below, above):
    below_across = send(across, 0, 1)
    above_across = send(across, 0, 3)
    far = send(below, 0, 1)
    far_across = send(above_across, 0, 3)
    return (own, across, below, below_across, above, above_across, far, far_across)


def exchange(value):
    return lax.all_to_all(
        value, "fsdp", split_axis=0, concat_axis=0, tiled=True, axis_index_groups=SAME_CORE
    )


def update(mine, theirs, weight, moment1, moment2, corr_one, corr_two):
    grad = mine + theirs.astype(F32)
    first = 0.9 * moment1.astype(F32) + 0.1 * grad
    second = 0.95 * moment2.astype(F32) + 0.05 * grad * grad
    wide = weight.astype(F32)
    return (
        wide - 0.05 * (first / corr_one / (jnp.sqrt(second / corr_two) + 1e-08) + 0.1 * wide)
    ).astype(BF16)


def before_gossip(act, gain, cot, weight, moment1, moment2, corr_one, corr_two, coords):
    pieces = other_hops(*first_hops(cot))
    normed = exchange(normed_columns(act, gain))
    weight_theirs = send(weight, 0, 0, 1)
    mine, theirs = grad_chunk(coords, normed, pieces)
    swapped = send(theirs, 0, 0, 1)
    updated = update(mine, swapped, weight, moment1, moment2, corr_one, corr_two)
    return pieces, weight_theirs, updated


def with_gossip(bit, pieces, weight_theirs, updated, act, gain, weight, coords):
    partner = gossip(updated, bit)
    dn = dnormed_part(coords, weight, weight_theirs, [pieces], [(0, weight.shape[1])], None, BF16)
    input_gradient = input_gradients(act, gain, exchange(dn))
    new_weight = (0.5 * (updated.astype(F32) + partner.astype(F32))).astype(BF16)
    return new_weight[None], input_gradient[None]


def on_device(activations, gain, cotangent, weight, moment1, moment2, step):
    index = lax.axis_index("fsdp")
    coords = jnp.stack([index // 8, (index // 2) % 4, index % 2]).astype(jnp.int32)
    count = (step + 1).astype(F32)
    corr_one = 1.0 - jnp.power(F32(0.9), count)
    corr_two = 1.0 - jnp.power(F32(0.95), count)
    levels = min(4, lax.axis_size("rep").bit_length() - 1)
    which = jnp.remainder(step, levels)
    act, cot, weight = activations[0], cotangent[0], weight[0]
    rest = (weight, moment1[0], moment2[0], corr_one, corr_two, coords)
    ready = before_gossip(act, gain, cot, *rest)
    return lax.switch(
        which, [partial(with_gossip, bit) for bit in range(levels)], *ready, act, gain, weight, coords
    )


def solution(mesh):
    placed = (
        P("rep", "fsdp", None),
        P("rep", None),
        P("rep", "fsdp", None),
        P("rep", "fsdp", None),
        P("rep", "fsdp", None),
        P("rep", "fsdp", None),
        P(),
    )
    return jax.shard_map(
        on_device,
        mesh=mesh,
        in_specs=placed,
        out_specs=(P("rep", "fsdp", None), P("rep", "fsdp", None)),
        check_vma=False,
    )
```

```python
from functools import partial

import jax
import jax.numpy as jnp
from jax import lax
from jax.experimental import pallas as pl
from jax.experimental.pallas import tpu as pltpu
from jax.sharding import PartitionSpec as P

BF16 = jnp.bfloat16
F32 = jnp.float32
CHIPS = 8
SAME_CORE = [[2 * chip + core for chip in range(CHIPS)] for core in range(2)]


def moves(dx, dy, dcore=0):
    pairs = []
    for index in range(2 * CHIPS):
        x, y, core = index >> 3, (index >> 1) & 3, index & 1
        target = (((x + dx) % 2) * 4 + (y + dy) % 4) * 2 + (core + dcore) % 2
        pairs.append((index, target))
    return pairs


def send(value, dx, dy, dcore=0):
    return lax.ppermute(value, "fsdp", moves(dx, dy, dcore))


def gossip(value, bit):
    pairs = [(source, source ^ (1 << bit)) for source in range(lax.axis_size("rep"))]
    return lax.ppermute(value, "rep", pairs)


def after(value, *others):
    return lax.optimization_barrier((value, *others))[0]


def norm_kernel(act_ref, gain_ref, out_ref):
    wide = act_ref[...].astype(F32)
    inverse = lax.rsqrt(jnp.mean(wide * wide, axis=-1, keepdims=True) + 1e-05)
    columns = out_ref.shape[1]
    for chip in range(CHIPS):
        part = pl.ds(chip * columns, columns)
        normed = act_ref[:, part].astype(F32) * inverse * gain_ref[:, part]
        out_ref[chip] = normed.T.astype(BF16)


def normed_columns(act, gain):
    tokens, width = act.shape
    return pl.pallas_call(
        norm_kernel,
        out_shape=jax.ShapeDtypeStruct((CHIPS, width // CHIPS, tokens), BF16),
        in_specs=[pl.BlockSpec(memory_space=pltpu.VMEM)] * 2,
        out_specs=pl.BlockSpec(memory_space=pltpu.VMEM),
        compiler_params=pltpu.CompilerParams(vmem_limit_bytes=10 * 2**20),
        cost_estimate=pl.CostEstimate(flops=8 * tokens * width, bytes_accessed=4 * tokens * width, transcendentals=0),
        name="norm",
    )(act, gain)


def places(coords_ref):
    x, y = coords_ref[0], coords_ref[1]
    return [
        ((x + dx) % 2) * 4 + (y + dy) % 4
        for dx, dy in ((0, 0), (1, 0), (0, 3), (1, 3), (0, 1), (1, 1), (0, 2), (1, 2))
    ]


NEAR = 6


def near_kernel(coords_ref, normed_ref, *refs):
    pieces, (sum_ref, lhs, rhs, sems) = refs[:NEAR], refs[NEAR:]
    tokens = pieces[0].shape[0]
    copies = []
    for at, block in enumerate(places(coords_ref)[:NEAR]):
        part = pl.ds(at * tokens, tokens)
        copies.append(pltpu.make_async_copy(normed_ref.at[block], lhs.at[:, part], sems.at[at]))
        copies.append(pltpu.make_async_copy(pieces[at], rhs.at[part], sems.at[NEAR + at]))
    for copy in copies:
        copy.start()
    for copy in copies:
        copy.wait()
    tile = 256

    @pl.loop(0, rhs.shape[1] // tile)
    def _(step):
        cols = pl.ds(pl.multiple_of(step * tile, tile), tile)
        sum_ref[:, cols] = jnp.dot(lhs[...], rhs[:, cols], preferred_element_type=F32)


def near_grad(coords, normed, pieces):
    tokens, width = pieces[0].shape
    columns = normed.shape[1]
    depth = NEAR * tokens
    return pl.pallas_call(
        near_kernel,
        out_shape=jax.ShapeDtypeStruct((columns, width), F32),
        in_specs=[pl.BlockSpec(memory_space=pltpu.SMEM)] + [pl.BlockSpec(memory_space=pltpu.HBM)] * (1 + NEAR),
        out_specs=pl.BlockSpec(memory_space=pltpu.VMEM),
        scratch_shapes=[
            pltpu.VMEM((columns, depth), BF16),
            pltpu.VMEM((depth, width), BF16),
            pltpu.SemaphoreType.DMA((2 * NEAR,)),
        ],
        compiler_params=pltpu.CompilerParams(vmem_limit_bytes=20 * 2**20),
        cost_estimate=pl.CostEstimate(
            flops=2 * depth * columns * width,
            bytes_accessed=2 * depth * (columns + width) + 4 * columns * width,
            transcendentals=0,
        ),
        name="near_grad",
    )(coords, normed, *pieces)


def far_kernel(coords_ref, normed_ref, one_ref, two_ref, sum_ref, own_ref, other_ref, lhs, rhs, total, sems):
    tokens, rows = one_ref.shape[0], own_ref.shape[0]
    core = coords_ref[2]

    @pl.when(pl.program_id(0) == 0)
    def _():
        copies = [
            pltpu.make_async_copy(normed_ref.at[block], lhs.at[:, pl.ds(at * tokens, tokens)], sems.at[at])
            for at, block in enumerate(places(coords_ref)[NEAR:])
        ]
        for copy in copies:
            copy.start()
        for copy in copies:
            copy.wait()

    rhs[:tokens] = one_ref[...]
    rhs[tokens:] = two_ref[...]
    total[...] = sum_ref[...] + jnp.dot(lhs[...], rhs[...], preferred_element_type=F32)
    own_ref[...] = total[pl.ds(pl.multiple_of(core * rows, rows), rows), :]
    other_ref[...] = total[pl.ds(pl.multiple_of((1 - core) * rows, rows), rows), :].astype(BF16)


def far_grad(coords, normed, pieces, near):
    tokens, width = pieces[0].shape
    columns = normed.shape[1]
    rows = columns // 2
    depth = len(pieces) * tokens
    tile = 512
    across = lambda height: pl.BlockSpec((height, tile), lambda i: (0, i))
    return pl.pallas_call(
        far_kernel,
        grid=(width // tile,),
        out_shape=(jax.ShapeDtypeStruct((rows, width), F32), jax.ShapeDtypeStruct((rows, width), BF16)),
        in_specs=[
            pl.BlockSpec(memory_space=pltpu.SMEM),
            pl.BlockSpec(memory_space=pltpu.HBM),
            across(tokens),
            across(tokens),
            across(columns),
        ],
        out_specs=(across(rows), across(rows)),
        scratch_shapes=[
            pltpu.VMEM((columns, depth), BF16),
            pltpu.VMEM((depth, tile), BF16),
            pltpu.VMEM((columns, tile), F32),
            pltpu.SemaphoreType.DMA((2,)),
        ],
        compiler_params=pltpu.CompilerParams(vmem_limit_bytes=20 * 2**20),
        cost_estimate=pl.CostEstimate(
            flops=2 * depth * columns * width,
            bytes_accessed=2 * depth * (columns + width) + 4 * columns * width + 6 * rows * width,
            transcendentals=0,
        ),
        name="far_grad",
    )(coords, normed, *pieces, near)


def dnormed_kernel(n_chunks, spans, carried, coords_ref, mine_ref, theirs_ref, *refs):
    n_pieces = n_chunks * CHIPS
    pieces, rest = refs[:n_pieces], refs[n_pieces:]
    if carried:
        sum_ref, rest = rest[0], rest[1:]
    out_ref, lhs, rhs, sems = rest
    tokens = pieces[0].shape[0]
    rows = mine_ref.shape[0]
    core = coords_ref[2]
    first, last = spans[0][0], spans[-1][1]
    copies = []
    for which, ref in enumerate((mine_ref, theirs_ref)):
        half = core if which == 0 else 1 - core
        start = pl.multiple_of(half * rows, rows)
        copies.append(
            pltpu.make_async_copy(ref.at[:, pl.ds(first, last - first)], rhs.at[pl.ds(start, rows)], sems.at[which])
        )
    for chunk, (low, high) in enumerate(spans):
        for at, block in enumerate(places(coords_ref)):
            number = chunk * CHIPS + at
            start = pl.multiple_of(block * tokens, tokens)
            copies.append(
                pltpu.make_async_copy(
                    pieces[number],
                    lhs.at[pl.ds(start, tokens), pl.ds(low - first, high - low)],
                    sems.at[2 + number],
                )
            )
    for copy in copies:
        copy.start()
    for copy in copies:
        copy.wait()

    @pl.loop(0, CHIPS // 2)
    def _(step):
        these = pl.ds(pl.multiple_of(step * 2 * tokens, 2 * tokens), 2 * tokens)
        part = lax.dot_general(lhs[these, :], rhs[...], (((1,), (1,)), ((), ())), preferred_element_type=F32)
        part = part.reshape(2, tokens, 2 * rows)
        blocks = pl.ds(step * 2, 2)
        if carried:
            part = part + sum_ref[blocks]
        out_ref[blocks] = part.astype(out_ref.dtype)


def dnormed_part(coords, mine, theirs, chunks, spans, carry, dtype):
    tokens = chunks[0][0].shape[0]
    rows = mine.shape[0]
    depth = spans[-1][1] - spans[0][0]
    pieces = [piece for chunk in chunks for piece in chunk]
    every = CHIPS * tokens
    vmem = pl.BlockSpec(memory_space=pltpu.VMEM)
    carried = [] if carry is None else [carry]
    return pl.pallas_call(
        partial(dnormed_kernel, len(chunks), spans, bool(carried)),
        out_shape=jax.ShapeDtypeStruct((CHIPS, tokens, 2 * rows), dtype),
        in_specs=[pl.BlockSpec(memory_space=pltpu.SMEM)]
        + [pl.BlockSpec(memory_space=pltpu.HBM)] * (2 + len(pieces))
        + [vmem] * len(carried),
        out_specs=vmem,
        scratch_shapes=[
            pltpu.VMEM((every, depth), BF16),
            pltpu.VMEM((2 * rows, depth), BF16),
            pltpu.SemaphoreType.DMA((2 + len(pieces),)),
        ],
        compiler_params=pltpu.CompilerParams(vmem_limit_bytes=20 * 2**20),
        cost_estimate=pl.CostEstimate(
            flops=4 * every * rows * depth,
            bytes_accessed=2 * (every + 2 * rows) * depth + 8 * every * rows,
            transcendentals=0,
        ),
        name="dnormed",
    )(coords, mine, theirs, *pieces, *carried)


def input_kernel(act_ref, gain_ref, dn_ref, out_ref):
    width = act_ref.shape[1]
    columns = dn_ref.shape[2]
    square = dot = 0.0
    for chip in range(CHIPS):
        part = pl.ds(chip * columns, columns)
        wide = act_ref[:, part].astype(F32)
        scaled = gain_ref[:, part] * dn_ref[chip].astype(F32)
        square = square + jnp.sum(wide * wide, axis=-1, keepdims=True)
        dot = dot + jnp.sum(scaled * wide, axis=-1, keepdims=True)
    inverse = lax.rsqrt(square / width + 1e-05)
    inner = inverse * dot / width
    for chip in range(CHIPS):
        part = pl.ds(chip * columns, columns)
        hat = act_ref[:, part].astype(F32) * inverse
        scaled = gain_ref[:, part] * dn_ref[chip].astype(F32)
        out_ref[:, part] = (inverse * (scaled - hat * inner)).astype(BF16)


def input_gradients(act, gain, dn):
    tokens, width = act.shape
    step = 32
    return pl.pallas_call(
        input_kernel,
        grid=(tokens // step,),
        out_shape=jax.ShapeDtypeStruct((tokens, width), BF16),
        in_specs=[
            pl.BlockSpec((step, width), lambda i: (i, 0)),
            pl.BlockSpec((1, width), lambda i: (0, 0)),
            pl.BlockSpec((CHIPS, step, width // CHIPS), lambda i: (0, i, 0)),
        ],
        out_specs=pl.BlockSpec((step, width), lambda i: (i, 0)),
        compiler_params=pltpu.CompilerParams(vmem_limit_bytes=8 * 2**20),
        cost_estimate=pl.CostEstimate(flops=12 * tokens * width, bytes_accessed=6 * tokens * width, transcendentals=0),
        name="input_gradient",
    )(act, gain, dn)


def first_hops(own):
    return own, send(own, 1, 0), send(own, 0, 1), send(own, 0, 3)


def other_hops(own, across, below, above):
    below_across = send(across, 0, 1)
    above_across = send(across, 0, 3)
    far = send(below, 0, 1)
    far_across = send(above_across, 0, 3)
    return (own, across, below, below_across, above, above_across, far, far_across)


def exchange(value):
    return lax.all_to_all(
        value, "fsdp", split_axis=0, concat_axis=0, tiled=True, axis_index_groups=SAME_CORE
    )


def update(mine, theirs, weight, moment1, moment2, corr_one, corr_two):
    grad = mine + theirs.astype(F32)
    first = 0.9 * moment1.astype(F32) + 0.1 * grad
    second = 0.95 * moment2.astype(F32) + 0.05 * grad * grad
    wide = weight.astype(F32)
    return (
        wide - 0.05 * (first / corr_one / (jnp.sqrt(second / corr_two) + 1e-08) + 0.1 * wide)
    ).astype(BF16)


def before_gossip(act, gain, cot, weight, moment1, moment2, corr_one, corr_two, coords):
    pieces = other_hops(*first_hops(cot))
    normed = exchange(normed_columns(act, gain))
    weight_theirs = send(weight, 0, 0, 1)
    near = near_grad(coords, normed, pieces[:NEAR])
    mine, theirs = far_grad(coords, normed, pieces[NEAR:], near)
    swapped = send(theirs, 0, 0, 1)
    updated = update(mine, swapped, weight, moment1, moment2, corr_one, corr_two)
    return pieces, weight_theirs, updated


def with_gossip(bit, pieces, weight_theirs, updated, act, gain, weight, coords):
    partner = gossip(updated, bit)
    dn = dnormed_part(coords, weight, weight_theirs, [pieces], [(0, weight.shape[1])], None, BF16)
    input_gradient = input_gradients(act, gain, exchange(dn))
    new_weight = (0.5 * (updated.astype(F32) + partner.astype(F32))).astype(BF16)
    return new_weight[None], input_gradient[None]


def on_device(activations, gain, cotangent, weight, moment1, moment2, step):
    index = lax.axis_index("fsdp")
    coords = jnp.stack([index // 8, (index // 2) % 4, index % 2]).astype(jnp.int32)
    count = (step + 1).astype(F32)
    corr_one = 1.0 - jnp.power(F32(0.9), count)
    corr_two = 1.0 - jnp.power(F32(0.95), count)
    levels = min(4, lax.axis_size("rep").bit_length() - 1)
    which = jnp.remainder(step, levels)
    act, cot, weight = activations[0], cotangent[0], weight[0]
    rest = (weight, moment1[0], moment2[0], corr_one, corr_two, coords)
    ready = before_gossip(act, gain, cot, *rest)
    return lax.switch(
        which, [partial(with_gossip, bit) for bit in range(levels)], *ready, act, gain, weight, coords
    )


def solution(mesh):
    placed = (
        P("rep", "fsdp", None),
        P("rep", None),
        P("rep", "fsdp", None),
        P("rep", "fsdp", None),
        P("rep", "fsdp", None),
        P("rep", "fsdp", None),
        P(),
    )
    return jax.shard_map(
        on_device,
        mesh=mesh,
        in_specs=placed,
        out_specs=(P("rep", "fsdp", None), P("rep", "fsdp", None)),
        check_vma=False,
    )
```

```python
from functools import partial

import jax
import jax.numpy as jnp
from jax import lax
from jax.experimental import pallas as pl
from jax.experimental.pallas import tpu as pltpu
from jax.sharding import PartitionSpec as P

BF16 = jnp.bfloat16
F32 = jnp.float32
CHIPS = 8
SAME_CORE = [[2 * chip + core for chip in range(CHIPS)] for core in range(2)]


def moves(dx, dy, dcore=0):
    pairs = []
    for index in range(2 * CHIPS):
        x, y, core = index >> 3, (index >> 1) & 3, index & 1
        target = (((x + dx) % 2) * 4 + (y + dy) % 4) * 2 + (core + dcore) % 2
        pairs.append((index, target))
    return pairs


def send(value, dx, dy, dcore=0):
    return lax.ppermute(value, "fsdp", moves(dx, dy, dcore))


def gossip(value, bit):
    pairs = [(source, source ^ (1 << bit)) for source in range(lax.axis_size("rep"))]
    return lax.ppermute(value, "rep", pairs)


def after(value, *others):
    return lax.optimization_barrier((value, *others))[0]


def norm_kernel(act_ref, gain_ref, out_ref):
    wide = act_ref[...].astype(F32)
    inverse = lax.rsqrt(jnp.mean(wide * wide, axis=-1, keepdims=True) + 1e-05)
    columns = out_ref.shape[1]
    for chip in range(CHIPS):
        part = pl.ds(chip * columns, columns)
        normed = act_ref[:, part].astype(F32) * inverse * gain_ref[:, part]
        out_ref[chip] = normed.T.astype(BF16)


def normed_columns(act, gain):
    tokens, width = act.shape
    return pl.pallas_call(
        norm_kernel,
        out_shape=jax.ShapeDtypeStruct((CHIPS, width // CHIPS, tokens), BF16),
        in_specs=[pl.BlockSpec(memory_space=pltpu.VMEM)] * 2,
        out_specs=pl.BlockSpec(memory_space=pltpu.VMEM),
        compiler_params=pltpu.CompilerParams(vmem_limit_bytes=10 * 2**20),
        cost_estimate=pl.CostEstimate(flops=8 * tokens * width, bytes_accessed=4 * tokens * width, transcendentals=0),
        name="norm",
    )(act, gain)


def places(coords_ref):
    x, y = coords_ref[0], coords_ref[1]
    return [
        ((x + dx) % 2) * 4 + (y + dy) % 4
        for dx, dy in ((0, 0), (1, 0), (0, 3), (1, 3), (0, 1), (1, 1), (0, 2), (1, 2))
    ]


NEAR = 6


def near_kernel(coords_ref, normed_ref, *refs):
    pieces, (sum_ref, lhs, rhs, sems) = refs[:NEAR], refs[NEAR:]
    tokens = pieces[0].shape[0]
    copies = []
    for at, block in enumerate(places(coords_ref)[:NEAR]):
        part = pl.ds(at * tokens, tokens)
        copies.append(pltpu.make_async_copy(normed_ref.at[block], lhs.at[:, part], sems.at[at]))
        copies.append(pltpu.make_async_copy(pieces[at], rhs.at[part], sems.at[NEAR + at]))
    for copy in copies:
        copy.start()
    for copy in copies:
        copy.wait()
    tile = 256

    @pl.loop(0, rhs.shape[1] // tile)
    def _(step):
        cols = pl.ds(pl.multiple_of(step * tile, tile), tile)
        sum_ref[:, cols] = jnp.dot(lhs[...], rhs[:, cols], preferred_element_type=F32)


def near_grad(coords, normed, pieces):
    tokens, width = pieces[0].shape
    columns = normed.shape[1]
    depth = NEAR * tokens
    return pl.pallas_call(
        near_kernel,
        out_shape=jax.ShapeDtypeStruct((columns, width), F32),
        in_specs=[pl.BlockSpec(memory_space=pltpu.SMEM)] + [pl.BlockSpec(memory_space=pltpu.HBM)] * (1 + NEAR),
        out_specs=pl.BlockSpec(memory_space=pltpu.VMEM),
        scratch_shapes=[
            pltpu.VMEM((columns, depth), BF16),
            pltpu.VMEM((depth, width), BF16),
            pltpu.SemaphoreType.DMA((2 * NEAR,)),
        ],
        compiler_params=pltpu.CompilerParams(vmem_limit_bytes=20 * 2**20),
        cost_estimate=pl.CostEstimate(
            flops=2 * depth * columns * width,
            bytes_accessed=2 * depth * (columns + width) + 4 * columns * width,
            transcendentals=0,
        ),
        name="near_grad",
    )(coords, normed, *pieces)


def far_kernel(coords_ref, normed_ref, one_ref, two_ref, sum_ref, own_ref, other_ref, lhs, rhs, total, sems):
    tokens, rows = one_ref.shape[0], own_ref.shape[0]
    core = coords_ref[2]

    @pl.when(pl.program_id(0) == 0)
    def _():
        copies = [
            pltpu.make_async_copy(normed_ref.at[block], lhs.at[:, pl.ds(at * tokens, tokens)], sems.at[at])
            for at, block in enumerate(places(coords_ref)[NEAR:])
        ]
        for copy in copies:
            copy.start()
        for copy in copies:
            copy.wait()

    rhs[:tokens] = one_ref[...]
    rhs[tokens:] = two_ref[...]
    total[...] = sum_ref[...] + jnp.dot(lhs[...], rhs[...], preferred_element_type=F32)
    own_ref[...] = total[pl.ds(pl.multiple_of(core * rows, rows), rows), :]
    other_ref[...] = total[pl.ds(pl.multiple_of((1 - core) * rows, rows), rows), :].astype(BF16)


def far_grad(coords, normed, pieces, near):
    tokens, width = pieces[0].shape
    columns = normed.shape[1]
    rows = columns // 2
    depth = len(pieces) * tokens
    tile = 512
    across = lambda height: pl.BlockSpec((height, tile), lambda i: (0, i))
    return pl.pallas_call(
        far_kernel,
        grid=(width // tile,),
        out_shape=(jax.ShapeDtypeStruct((rows, width), F32), jax.ShapeDtypeStruct((rows, width), BF16)),
        in_specs=[
            pl.BlockSpec(memory_space=pltpu.SMEM),
            pl.BlockSpec(memory_space=pltpu.HBM),
            across(tokens),
            across(tokens),
            across(columns),
        ],
        out_specs=(across(rows), across(rows)),
        scratch_shapes=[
            pltpu.VMEM((columns, depth), BF16),
            pltpu.VMEM((depth, tile), BF16),
            pltpu.VMEM((columns, tile), F32),
            pltpu.SemaphoreType.DMA((2,)),
        ],
        compiler_params=pltpu.CompilerParams(vmem_limit_bytes=20 * 2**20),
        cost_estimate=pl.CostEstimate(
            flops=2 * depth * columns * width,
            bytes_accessed=2 * depth * (columns + width) + 4 * columns * width + 6 * rows * width,
            transcendentals=0,
        ),
        name="far_grad",
    )(coords, normed, *pieces, near)


def dnormed_kernel(n_chunks, spans, carried, coords_ref, mine_ref, theirs_ref, *refs):
    n_pieces = n_chunks * CHIPS
    pieces, rest = refs[:n_pieces], refs[n_pieces:]
    if carried:
        sum_ref, rest = rest[0], rest[1:]
    out_ref, lhs, rhs, sems = rest
    tokens = pieces[0].shape[0]
    rows = mine_ref.shape[0]
    core = coords_ref[2]
    first, last = spans[0][0], spans[-1][1]
    copies = []
    for which, ref in enumerate((mine_ref, theirs_ref)):
        half = core if which == 0 else 1 - core
        start = pl.multiple_of(half * rows, rows)
        copies.append(
            pltpu.make_async_copy(ref.at[:, pl.ds(first, last - first)], rhs.at[pl.ds(start, rows)], sems.at[which])
        )
    for chunk, (low, high) in enumerate(spans):
        for at, block in enumerate(places(coords_ref)):
            number = chunk * CHIPS + at
            start = pl.multiple_of(block * tokens, tokens)
            copies.append(
                pltpu.make_async_copy(
                    pieces[number],
                    lhs.at[pl.ds(start, tokens), pl.ds(low - first, high - low)],
                    sems.at[2 + number],
                )
            )
    for copy in copies:
        copy.start()
    for copy in copies:
        copy.wait()

    @pl.loop(0, CHIPS // 2)
    def _(step):
        these = pl.ds(pl.multiple_of(step * 2 * tokens, 2 * tokens), 2 * tokens)
        part = lax.dot_general(lhs[these, :], rhs[...], (((1,), (1,)), ((), ())), preferred_element_type=F32)
        part = part.reshape(2, tokens, 2 * rows)
        blocks = pl.ds(step * 2, 2)
        if carried:
            part = part + sum_ref[blocks]
        out_ref[blocks] = part.astype(out_ref.dtype)


def dnormed_part(coords, mine, theirs, chunks, spans, carry, dtype):
    tokens = chunks[0][0].shape[0]
    rows = mine.shape[0]
    depth = spans[-1][1] - spans[0][0]
    pieces = [piece for chunk in chunks for piece in chunk]
    every = CHIPS * tokens
    vmem = pl.BlockSpec(memory_space=pltpu.VMEM)
    carried = [] if carry is None else [carry]
    return pl.pallas_call(
        partial(dnormed_kernel, len(chunks), spans, bool(carried)),
        out_shape=jax.ShapeDtypeStruct((CHIPS, tokens, 2 * rows), dtype),
        in_specs=[pl.BlockSpec(memory_space=pltpu.SMEM)]
        + [pl.BlockSpec(memory_space=pltpu.HBM)] * (2 + len(pieces))
        + [vmem] * len(carried),
        out_specs=vmem,
        scratch_shapes=[
            pltpu.VMEM((every, depth), BF16),
            pltpu.VMEM((2 * rows, depth), BF16),
            pltpu.SemaphoreType.DMA((2 + len(pieces),)),
        ],
        compiler_params=pltpu.CompilerParams(vmem_limit_bytes=20 * 2**20),
        cost_estimate=pl.CostEstimate(
            flops=4 * every * rows * depth,
            bytes_accessed=2 * (every + 2 * rows) * depth + 8 * every * rows,
            transcendentals=0,
        ),
        name="dnormed",
    )(coords, mine, theirs, *pieces, *carried)


def input_kernel(act_ref, gain_ref, dn_ref, out_ref):
    width = act_ref.shape[1]
    columns = dn_ref.shape[2]
    square = dot = 0.0
    for chip in range(CHIPS):
        part = pl.ds(chip * columns, columns)
        wide = act_ref[:, part].astype(F32)
        scaled = gain_ref[:, part] * dn_ref[chip].astype(F32)
        square = square + jnp.sum(wide * wide, axis=-1, keepdims=True)
        dot = dot + jnp.sum(scaled * wide, axis=-1, keepdims=True)
    inverse = lax.rsqrt(square / width + 1e-05)
    inner = inverse * dot / width
    for chip in range(CHIPS):
        part = pl.ds(chip * columns, columns)
        hat = act_ref[:, part].astype(F32) * inverse
        scaled = gain_ref[:, part] * dn_ref[chip].astype(F32)
        out_ref[:, part] = (inverse * (scaled - hat * inner)).astype(BF16)


def input_gradients(act, gain, dn):
    tokens, width = act.shape
    step = 32
    return pl.pallas_call(
        input_kernel,
        grid=(tokens // step,),
        out_shape=jax.ShapeDtypeStruct((tokens, width), BF16),
        in_specs=[
            pl.BlockSpec((step, width), lambda i: (i, 0)),
            pl.BlockSpec((1, width), lambda i: (0, 0)),
            pl.BlockSpec((CHIPS, step, width // CHIPS), lambda i: (0, i, 0)),
        ],
        out_specs=pl.BlockSpec((step, width), lambda i: (i, 0)),
        compiler_params=pltpu.CompilerParams(vmem_limit_bytes=8 * 2**20),
        cost_estimate=pl.CostEstimate(flops=12 * tokens * width, bytes_accessed=6 * tokens * width, transcendentals=0),
        name="input_gradient",
    )(act, gain, dn)


def first_hops(own):
    return own, send(own, 1, 0), send(own, 0, 1), send(own, 0, 3)


def other_hops(own, across, below, above):
    ready = after(across, below, above)
    below_across = send(ready, 0, 1)
    above_across = send(ready, 0, 3)
    far = send(below, 0, 1)
    far_across = send(above_across, 0, 3)
    return (own, across, below, below_across, above, above_across, far, far_across)


def exchange(value):
    return lax.all_to_all(
        value, "fsdp", split_axis=0, concat_axis=0, tiled=True, axis_index_groups=SAME_CORE
    )


def update(mine, theirs, weight, moment1, moment2, corr_one, corr_two):
    grad = mine + theirs.astype(F32)
    first = 0.9 * moment1.astype(F32) + 0.1 * grad
    second = 0.95 * moment2.astype(F32) + 0.05 * grad * grad
    wide = weight.astype(F32)
    return (
        wide - 0.05 * (first / corr_one / (jnp.sqrt(second / corr_two) + 1e-08) + 0.1 * wide)
    ).astype(BF16)


def before_gossip(act, gain, cot, weight, moment1, moment2, corr_one, corr_two, coords):
    pieces = other_hops(*first_hops(cot))
    normed = exchange(normed_columns(act, gain))
    weight_theirs = send(weight, 0, 0, 1)
    near = near_grad(coords, after(normed, weight_theirs), pieces[:NEAR])
    mine, theirs = far_grad(coords, normed, pieces[NEAR:], near)
    swapped = send(theirs, 0, 0, 1)
    updated = update(mine, swapped, weight, moment1, moment2, corr_one, corr_two)
    return pieces, weight_theirs, updated


def with_gossip(bit, pieces, weight_theirs, updated, act, gain, weight, coords):
    partner = gossip(updated, bit)
    dn = dnormed_part(coords, weight, weight_theirs, [pieces], [(0, weight.shape[1])], None, BF16)
    input_gradient = input_gradients(act, gain, exchange(dn))
    new_weight = (0.5 * (updated.astype(F32) + partner.astype(F32))).astype(BF16)
    return new_weight[None], input_gradient[None]


def on_device(activations, gain, cotangent, weight, moment1, moment2, step):
    index = lax.axis_index("fsdp")
    coords = jnp.stack([index // 8, (index // 2) % 4, index % 2]).astype(jnp.int32)
    count = (step + 1).astype(F32)
    corr_one = 1.0 - jnp.power(F32(0.9), count)
    corr_two = 1.0 - jnp.power(F32(0.95), count)
    levels = min(4, lax.axis_size("rep").bit_length() - 1)
    which = jnp.remainder(step, levels)
    act, cot, weight = activations[0], cotangent[0], weight[0]
    rest = (weight, moment1[0], moment2[0], corr_one, corr_two, coords)
    ready = before_gossip(act, gain, cot, *rest)
    return lax.switch(
        which, [partial(with_gossip, bit) for bit in range(levels)], *ready, act, gain, weight, coords
    )


def solution(mesh):
    placed = (
        P("rep", "fsdp", None),
        P("rep", None),
        P("rep", "fsdp", None),
        P("rep", "fsdp", None),
        P("rep", "fsdp", None),
        P("rep", "fsdp", None),
        P(),
    )
    return jax.shard_map(
        on_device,
        mesh=mesh,
        in_specs=placed,
        out_specs=(P("rep", "fsdp", None), P("rep", "fsdp", None)),
        check_vma=False,
    )
```

```python
from functools import partial

import jax
import jax.numpy as jnp
from jax import lax
from jax.experimental import pallas as pl
from jax.experimental.pallas import tpu as pltpu
from jax.sharding import PartitionSpec as P

BF16 = jnp.bfloat16
F32 = jnp.float32
CHIPS = 8
SAME_CORE = [[2 * chip + core for chip in range(CHIPS)] for core in range(2)]


def moves(dx, dy, dcore=0):
    pairs = []
    for index in range(2 * CHIPS):
        x, y, core = index >> 3, (index >> 1) & 3, index & 1
        target = (((x + dx) % 2) * 4 + (y + dy) % 4) * 2 + (core + dcore) % 2
        pairs.append((index, target))
    return pairs


def send(value, dx, dy, dcore=0):
    return lax.ppermute(value, "fsdp", moves(dx, dy, dcore))


def gossip(value, bit):
    pairs = [(source, source ^ (1 << bit)) for source in range(lax.axis_size("rep"))]
    return lax.ppermute(value, "rep", pairs)


def after(value, *others):
    return lax.optimization_barrier((value, *others))[0]


def norm_kernel(act_ref, gain_ref, out_ref):
    wide = act_ref[...].astype(F32)
    inverse = lax.rsqrt(jnp.mean(wide * wide, axis=-1, keepdims=True) + 1e-05)
    columns = out_ref.shape[1]
    for chip in range(CHIPS):
        part = pl.ds(chip * columns, columns)
        normed = act_ref[:, part].astype(F32) * inverse * gain_ref[:, part]
        out_ref[chip] = normed.T.astype(BF16)


def normed_columns(act, gain):
    tokens, width = act.shape
    return pl.pallas_call(
        norm_kernel,
        out_shape=jax.ShapeDtypeStruct((CHIPS, width // CHIPS, tokens), BF16),
        in_specs=[pl.BlockSpec(memory_space=pltpu.VMEM)] * 2,
        out_specs=pl.BlockSpec(memory_space=pltpu.VMEM),
        compiler_params=pltpu.CompilerParams(vmem_limit_bytes=10 * 2**20),
        cost_estimate=pl.CostEstimate(flops=8 * tokens * width, bytes_accessed=4 * tokens * width, transcendentals=0),
        name="norm",
    )(act, gain)


def places(coords_ref):
    x, y = coords_ref[0], coords_ref[1]
    return [
        ((x + dx) % 2) * 4 + (y + dy) % 4
        for dx, dy in ((0, 0), (1, 0), (0, 3), (1, 3), (0, 1), (1, 1), (0, 2), (1, 2))
    ]


NEAR = 6


def near_kernel(coords_ref, normed_ref, *refs):
    pieces, (sum_ref, lhs, rhs, sems) = refs[:NEAR], refs[NEAR:]
    tokens = pieces[0].shape[0]
    copies = []
    for at, block in enumerate(places(coords_ref)[:NEAR]):
        part = pl.ds(at * tokens, tokens)
        copies.append(pltpu.make_async_copy(normed_ref.at[block], lhs.at[:, part], sems.at[at]))
        copies.append(pltpu.make_async_copy(pieces[at], rhs.at[part], sems.at[NEAR + at]))
    for copy in copies:
        copy.start()
    for copy in copies:
        copy.wait()
    tile = 256

    @pl.loop(0, rhs.shape[1] // tile)
    def _(step):
        cols = pl.ds(pl.multiple_of(step * tile, tile), tile)
        sum_ref[:, cols] = jnp.dot(lhs[...], rhs[:, cols], preferred_element_type=F32)


def near_grad(coords, normed, pieces):
    tokens, width = pieces[0].shape
    columns = normed.shape[1]
    depth = NEAR * tokens
    return pl.pallas_call(
        near_kernel,
        out_shape=jax.ShapeDtypeStruct((columns, width), F32),
        in_specs=[pl.BlockSpec(memory_space=pltpu.SMEM)] + [pl.BlockSpec(memory_space=pltpu.HBM)] * (1 + NEAR),
        out_specs=pl.BlockSpec(memory_space=pltpu.VMEM),
        scratch_shapes=[
            pltpu.VMEM((columns, depth), BF16),
            pltpu.VMEM((depth, width), BF16),
            pltpu.SemaphoreType.DMA((2 * NEAR,)),
        ],
        compiler_params=pltpu.CompilerParams(vmem_limit_bytes=20 * 2**20),
        cost_estimate=pl.CostEstimate(
            flops=2 * depth * columns * width,
            bytes_accessed=2 * depth * (columns + width) + 4 * columns * width,
            transcendentals=0,
        ),
        name="near_grad",
    )(coords, normed, *pieces)


def far_kernel(coords_ref, normed_ref, one_ref, two_ref, sum_ref, own_ref, other_ref, lhs, rhs, total, sems):
    tokens, rows = one_ref.shape[0], own_ref.shape[0]
    core = coords_ref[2]

    @pl.when(pl.program_id(0) == 0)
    def _():
        copies = [
            pltpu.make_async_copy(normed_ref.at[block], lhs.at[:, pl.ds(at * tokens, tokens)], sems.at[at])
            for at, block in enumerate(places(coords_ref)[NEAR:])
        ]
        for copy in copies:
            copy.start()
        for copy in copies:
            copy.wait()

    rhs[:tokens] = one_ref[...]
    rhs[tokens:] = two_ref[...]
    total[...] = sum_ref[...] + jnp.dot(lhs[...], rhs[...], preferred_element_type=F32)
    own_ref[...] = total[pl.ds(pl.multiple_of(core * rows, rows), rows), :]
    other_ref[...] = total[pl.ds(pl.multiple_of((1 - core) * rows, rows), rows), :].astype(BF16)


def far_grad(coords, normed, pieces, near):
    tokens, width = pieces[0].shape
    columns = normed.shape[1]
    rows = columns // 2
    depth = len(pieces) * tokens
    tile = 512
    across = lambda height: pl.BlockSpec((height, tile), lambda i: (0, i))
    return pl.pallas_call(
        far_kernel,
        grid=(width // tile,),
        out_shape=(jax.ShapeDtypeStruct((rows, width), F32), jax.ShapeDtypeStruct((rows, width), BF16)),
        in_specs=[
            pl.BlockSpec(memory_space=pltpu.SMEM),
            pl.BlockSpec(memory_space=pltpu.HBM),
            across(tokens),
            across(tokens),
            across(columns),
        ],
        out_specs=(across(rows), across(rows)),
        scratch_shapes=[
            pltpu.VMEM((columns, depth), BF16),
            pltpu.VMEM((depth, tile), BF16),
            pltpu.VMEM((columns, tile), F32),
            pltpu.SemaphoreType.DMA((2,)),
        ],
        compiler_params=pltpu.CompilerParams(vmem_limit_bytes=20 * 2**20),
        cost_estimate=pl.CostEstimate(
            flops=2 * depth * columns * width,
            bytes_accessed=2 * depth * (columns + width) + 4 * columns * width + 6 * rows * width,
            transcendentals=0,
        ),
        name="far_grad",
    )(coords, normed, *pieces, near)


def dnormed_kernel(n_chunks, spans, carried, coords_ref, mine_ref, theirs_ref, *refs):
    n_pieces = n_chunks * CHIPS
    pieces, rest = refs[:n_pieces], refs[n_pieces:]
    if carried:
        sum_ref, rest = rest[0], rest[1:]
    out_ref, lhs, rhs, sems = rest
    tokens = pieces[0].shape[0]
    rows = mine_ref.shape[0]
    core = coords_ref[2]
    first, last = spans[0][0], spans[-1][1]
    copies = []
    for which, ref in enumerate((mine_ref, theirs_ref)):
        half = core if which == 0 else 1 - core
        start = pl.multiple_of(half * rows, rows)
        copies.append(
            pltpu.make_async_copy(ref.at[:, pl.ds(first, last - first)], rhs.at[pl.ds(start, rows)], sems.at[which])
        )
    for chunk, (low, high) in enumerate(spans):
        for at, block in enumerate(places(coords_ref)):
            number = chunk * CHIPS + at
            start = pl.multiple_of(block * tokens, tokens)
            copies.append(
                pltpu.make_async_copy(
                    pieces[number],
                    lhs.at[pl.ds(start, tokens), pl.ds(low - first, high - low)],
                    sems.at[2 + number],
                )
            )
    for copy in copies:
        copy.start()
    for copy in copies:
        copy.wait()

    @pl.loop(0, CHIPS // 2)
    def _(step):
        these = pl.ds(pl.multiple_of(step * 2 * tokens, 2 * tokens), 2 * tokens)
        part = lax.dot_general(lhs[these, :], rhs[...], (((1,), (1,)), ((), ())), preferred_element_type=F32)
        part = part.reshape(2, tokens, 2 * rows)
        blocks = pl.ds(step * 2, 2)
        if carried:
            part = part + sum_ref[blocks]
        out_ref[blocks] = part.astype(out_ref.dtype)


def dnormed_part(coords, mine, theirs, chunks, spans, carry, dtype):
    tokens = chunks[0][0].shape[0]
    rows = mine.shape[0]
    depth = spans[-1][1] - spans[0][0]
    pieces = [piece for chunk in chunks for piece in chunk]
    every = CHIPS * tokens
    vmem = pl.BlockSpec(memory_space=pltpu.VMEM)
    carried = [] if carry is None else [carry]
    return pl.pallas_call(
        partial(dnormed_kernel, len(chunks), spans, bool(carried)),
        out_shape=jax.ShapeDtypeStruct((CHIPS, tokens, 2 * rows), dtype),
        in_specs=[pl.BlockSpec(memory_space=pltpu.SMEM)]
        + [pl.BlockSpec(memory_space=pltpu.HBM)] * (2 + len(pieces))
        + [vmem] * len(carried),
        out_specs=vmem,
        scratch_shapes=[
            pltpu.VMEM((every, depth), BF16),
            pltpu.VMEM((2 * rows, depth), BF16),
            pltpu.SemaphoreType.DMA((2 + len(pieces),)),
        ],
        compiler_params=pltpu.CompilerParams(vmem_limit_bytes=20 * 2**20),
        cost_estimate=pl.CostEstimate(
            flops=4 * every * rows * depth,
            bytes_accessed=2 * (every + 2 * rows) * depth + 8 * every * rows,
            transcendentals=0,
        ),
        name="dnormed",
    )(coords, mine, theirs, *pieces, *carried)


def input_kernel(act_ref, gain_ref, dn_ref, out_ref):
    width = act_ref.shape[1]
    columns = dn_ref.shape[2]
    square = dot = 0.0
    for chip in range(CHIPS):
        part = pl.ds(chip * columns, columns)
        wide = act_ref[:, part].astype(F32)
        scaled = gain_ref[:, part] * dn_ref[chip].astype(F32)
        square = square + jnp.sum(wide * wide, axis=-1, keepdims=True)
        dot = dot + jnp.sum(scaled * wide, axis=-1, keepdims=True)
    inverse = lax.rsqrt(square / width + 1e-05)
    inner = inverse * dot / width
    for chip in range(CHIPS):
        part = pl.ds(chip * columns, columns)
        hat = act_ref[:, part].astype(F32) * inverse
        scaled = gain_ref[:, part] * dn_ref[chip].astype(F32)
        out_ref[:, part] = (inverse * (scaled - hat * inner)).astype(BF16)


def input_gradients(act, gain, dn):
    tokens, width = act.shape
    step = 32
    return pl.pallas_call(
        input_kernel,
        grid=(tokens // step,),
        out_shape=jax.ShapeDtypeStruct((tokens, width), BF16),
        in_specs=[
            pl.BlockSpec((step, width), lambda i: (i, 0)),
            pl.BlockSpec((1, width), lambda i: (0, 0)),
            pl.BlockSpec((CHIPS, step, width // CHIPS), lambda i: (0, i, 0)),
        ],
        out_specs=pl.BlockSpec((step, width), lambda i: (i, 0)),
        compiler_params=pltpu.CompilerParams(vmem_limit_bytes=8 * 2**20),
        cost_estimate=pl.CostEstimate(flops=12 * tokens * width, bytes_accessed=6 * tokens * width, transcendentals=0),
        name="input_gradient",
    )(act, gain, dn)


def first_hops(own):
    return own, send(own, 1, 0), send(own, 0, 1), send(own, 0, 3)


def other_hops(own, across, below, above):
    ready = after(across, below, above)
    below_across = send(ready, 0, 1)
    above_across = send(after(above, across, below), 1, 0)
    far = send(below, 0, 1)
    far_across = send(above_across, 0, 3)
    return (own, across, below, below_across, above, above_across, far, far_across)


def exchange(value):
    return lax.all_to_all(
        value, "fsdp", split_axis=0, concat_axis=0, tiled=True, axis_index_groups=SAME_CORE
    )


def update(mine, theirs, weight, moment1, moment2, corr_one, corr_two):
    grad = mine + theirs.astype(F32)
    first = 0.9 * moment1.astype(F32) + 0.1 * grad
    second = 0.95 * moment2.astype(F32) + 0.05 * grad * grad
    scaled = second * (1.0 / corr_two)
    root = scaled * lax.rsqrt(scaled)
    wide = weight.astype(F32)
    return (
        wide - 0.05 * (first * (1.0 / corr_one) / (root + 1e-08) + 0.1 * wide)
    ).astype(BF16)


def before_gossip(act, gain, cot, weight, moment1, moment2, corr_one, corr_two, coords):
    pieces = other_hops(*first_hops(cot))
    normed = exchange(normed_columns(act, gain))
    weight_theirs = send(weight, 0, 0, 1)
    near = near_grad(coords, after(normed, weight_theirs), pieces[:NEAR])
    mine, theirs = far_grad(coords, normed, pieces[NEAR:], near)
    swapped = send(theirs, 0, 0, 1)
    updated = update(mine, swapped, weight, moment1, moment2, corr_one, corr_two)
    return pieces, weight_theirs, updated


def with_gossip(bit, pieces, weight_theirs, updated, act, gain, weight, coords):
    partner = gossip(updated, bit)
    dn = dnormed_part(coords, weight, weight_theirs, [pieces], [(0, weight.shape[1])], None, BF16)
    input_gradient = input_gradients(act, gain, exchange(dn))
    new_weight = (0.5 * (updated.astype(F32) + partner.astype(F32))).astype(BF16)
    return new_weight[None], input_gradient[None]


def on_device(activations, gain, cotangent, weight, moment1, moment2, step):
    index = lax.axis_index("fsdp")
    coords = jnp.stack([index // 8, (index // 2) % 4, index % 2]).astype(jnp.int32)
    count = (step + 1).astype(F32)
    corr_one = 1.0 - jnp.power(F32(0.9), count)
    corr_two = 1.0 - jnp.power(F32(0.95), count)
    levels = min(4, lax.axis_size("rep").bit_length() - 1)
    which = jnp.remainder(step, levels)
    act, cot, weight = activations[0], cotangent[0], weight[0]
    rest = (weight, moment1[0], moment2[0], corr_one, corr_two, coords)
    ready = before_gossip(act, gain, cot, *rest)
    return lax.switch(
        which, [partial(with_gossip, bit) for bit in range(levels)], *ready, act, gain, weight, coords
    )


def solution(mesh):
    placed = (
        P("rep", "fsdp", None),
        P("rep", None),
        P("rep", "fsdp", None),
        P("rep", "fsdp", None),
        P("rep", "fsdp", None),
        P("rep", "fsdp", None),
        P(),
    )
    return jax.shard_map(
        on_device,
        mesh=mesh,
        in_specs=placed,
        out_specs=(P("rep", "fsdp", None), P("rep", "fsdp", None)),
        check_vma=False,
    )
```
